256 devices in a mesh: blk: 32 (over x, z), term: 8 (over y, core).
Axes of the slice: x: 4, y: 4, z: 8, core: 2. Of those that a mesh axis runs over, the one named last changes fastest.
Arguments:
- wave: float32 [8192, 8192], P('blk'), may hold values from -6 to 6
- left_env: float32 [8, 32, 256, 256], P('term', 'blk'), may hold values from -0.375 to 0.375
- right_env: float32 [8, 32, 256, 256], P('term', 'blk'), may hold values from -0.375 to 0.375
- left_dims: int32 [32], replicated, may hold values from 1 to 256, 4096 in all
- right_dims: int32 [32], replicated, may hold values from 1 to 256, 4096 in all
Outputs:
- applied: float32 [8192, 8192], P('term', 'blk')
The draws below stay inside these ranges and needn't reach their ends.
Inputs may be any that keep to these rules, and one draw needn't show every extreme that they name: `left_dims`: each sector dimension is at least 1 and at most 256; some sector has exactly 256; the dims of one side sum to 4096. `right_dims`: as for left_dims.
All inputs are finite; a program needn't handle non-finite values.
Results may differ from the reference program's by a relative error of at most 0.0001.
Values sent between devices are 32-bit elements; how exact they have to be, the bound alone decides.
A program may use at most 128 MiB of HBM per device.

```python
import math
import jax
import jax.numpy as jnp
import numpy as np
from jax import lax

SECTOR = 256
SECTORS = 32
BOND = 8192
TERMS = 8


def levels(own_key, shape, cuts, least, high):
    gain = 1.0
    for axis_at, shards_of in cuts:
        steps = jax.random.uniform(jax.random.fold_in(jax.random.fold_in(own_key, 6), axis_at), (shards_of,), jnp.float32, least / len(cuts), high / len(cuts))
        gain = gain * jnp.repeat(jnp.exp(steps), shape[axis_at] // shards_of).reshape((-1,) + (1,) * (len(shape) - 1 - axis_at))
    return gain


def split_up(amount, total, most, lean):
    weights = [(1 << 20) // math.isqrt(rank ** lean) + 1 for rank in range(2, amount + 1)]
    spare, counts = total - most - (amount - 1), [1] * (amount - 1)
    while spare > 0:
        movable = [i for i in range(amount - 1) if counts[i] < most]
        pool, remaining = sum([weights[i] for i in movable]), spare
        for i in movable:
            more = min(most - counts[i], max(1, remaining * weights[i] // pool), spare)
            counts[i] = counts[i] + more
            spare = spare - more
    return np.array([most] + counts)


def ragged_sizes(own_key, count, total, limit, slope):
    if count == 2:
        one = jax.random.randint(own_key, (), max(1, total - limit), min(limit, total - 1) + 1)
        return jnp.stack([one, total - one])
    tallies = jnp.asarray(split_up(count, total, limit, slope), jnp.int32)
    pairs = (count - 1) // 2
    source_of, receiver = tallies[1:1 + 2 * pairs:2], tallies[2:2 + 2 * pairs:2]
    slack = jnp.minimum(source_of - 1, limit - receiver)
    moved = jax.random.randint(jax.random.fold_in(own_key, 1), (pairs,), 0, 1 << 20) % (slack + 1)
    tallies = tallies.at[1:1 + 2 * pairs:2].set(source_of - moved).at[2:2 + 2 * pairs:2].set(receiver + moved)
    return tallies[jax.random.permutation(jax.random.fold_in(own_key, 2), count)]


def gaussian(stream_key, shape, spread, bound, shards=(), kind=jnp.bfloat16):
    factor_of = levels(stream_key, shape, shards, -0.22, 0.18) if shards else 1.0
    drawn = jax.random.normal(stream_key, shape, jnp.float32) * spread * factor_of
    return jnp.minimum(jnp.maximum(drawn, -bound), bound).astype(kind)


def setup_inputs(seed: int = 0) -> dict:
    key_list = jax.random.split(jax.random.key(seed), 6)
    return {
        "wave": gaussian(key_list[0], (BOND, BOND), 1.0, 6.0, ((0, 32),), jnp.float32),
        "left_env": gaussian(key_list[1], (TERMS, SECTORS, SECTOR, SECTOR), SECTOR ** -0.5, 0.375, ((0, 8), (1, 32)), jnp.float32),
        "right_env": gaussian(key_list[2], (TERMS, SECTORS, SECTOR, SECTOR), SECTOR ** -0.5, 0.375, ((0, 8), (1, 32)), jnp.float32),
        "left_dims": ragged_sizes(key_list[3], SECTORS, SECTORS * SECTOR // 2, SECTOR, 0).astype(jnp.int32),
        "right_dims": ragged_sizes(key_list[4], SECTORS, SECTORS * SECTOR // 2, SECTOR, 1).astype(jnp.int32),
    }


def sector_mask(dims):
    inside = jnp.arange(SECTOR, dtype=jnp.int32)[None, :] < dims[:, None]
    return inside.astype(jnp.float32).reshape(-1)


def reference(wave, left_env, right_env, left_dims, right_dims):
    row_mask = sector_mask(left_dims)
    col_mask = sector_mask(right_dims)
    masked = wave * row_mask[:, None] * col_mask[None, :]
    blocks = masked.reshape(SECTORS, SECTOR, BOND)
    total = jnp.zeros((BOND, BOND), jnp.float32)
    for term_k in range(TERMS):
        left_part = jnp.einsum("sab,sbc->sac", left_env[term_k], blocks, precision=lax.Precision.HIGHEST)
        left_part = left_part.reshape(BOND, SECTORS, SECTOR)
        product = jnp.einsum("rsb,sab->rsa", left_part, right_env[term_k], precision=lax.Precision.HIGHEST)
        total = total + product.reshape(BOND, BOND)
    return total * row_mask[:, None] * col_mask[None, :]
```

```python
import jax
import jax.numpy as jnp
from jax import lax
from jax.experimental import pallas as pl
from jax.experimental.pallas import tpu as pltpu
from jax.sharding import PartitionSpec as P

X, Y, Z = 4, 4, 8
SEC = 256
HALF = SEC // 2
RA = 192
RB = SEC - RA
CHUNKS = 16
EARLY = 6
LAG = 6
F32, BF16 = jnp.float32, jnp.bfloat16
MESH = pl.DeviceIdType.MESH


def device(x, y, z, c):
    return {"blk": x * Z + z, "term": y * 2 + c}


def rem(a, n):
    return lax.rem(a, jnp.int32(n))


def div(a, n):
    return lax.div(a, jnp.int32(n))


def split(a):
    high = a.astype(BF16)
    return high, (a - high.astype(F32)).astype(BF16)


def dot3(a, b, dims):
    (ah, al), (bh, bl) = a, b
    out = lax.dot_general(ah, bh, (dims, ((), ())), preferred_element_type=F32)
    out += lax.dot_general(ah, bl, (dims, ((), ())), preferred_element_type=F32)
    return out + lax.dot_general(al, bh, (dims, ((), ())), preferred_element_type=F32)


def received(ref, sem):
    pltpu.make_async_copy(ref, ref, sem).wait()


def kernel(
    ldims, rdims, wave, left, right, out,
    lbuf, rbuf, wbuf, wh, wl, rh, rl, acc,
    l1_s, ring_s, sib_s, l_r, sib_r,
    ra1_s, ra2_s, ra_r, rb1_s, rb1_r, rb2_s, rb2_r,
    w_s, w_r, o_s, o_r,
):
    blk, term = lax.axis_index("blk"), lax.axis_index("term")
    x, z = div(blk, Z), rem(blk, Z)
    y, c = div(term, 2), rem(term, 2)
    zpair, odd = div(z, 2), rem(z, 2)
    xpair, xodd = div(x, 2), rem(x, 2)
    ypair, yodd = div(y, 2), rem(y, 2)
    sibling = device(x, y, z, 1 - c)
    r_owner = c == xpair

    home = rem(z + 2 * rem(y + 2 * odd + c, 4), Z)
    l1_self = (zpair == y) & (home == z)
    l1_to = device(x, zpair, home, c)

    def term_pair(zh, core):
        return rem(div(zh, 2) - y - 2 * rem(zh, 2) - core + 8, 4)

    l1_from = device(x, term_pair(z, c), 2 * y + odd, c)

    def w_to(j):
        return device(x, zpair, rem(z + j, Z), ypair)

    def w_from(i):
        return device(x, 2 * c + i // 4, 2 * y + (i // 2) % 2, i % 2)

    w_self = (zpair == y) & (ypair == c)

    bar = pltpu.get_barrier_semaphore()

    def hello(target):
        pl.semaphore_signal(bar, inc=1, device_id=target, device_id_type=MESH)

    def hello_plane(i, carry):
        hello(device(rem(x + div(i, 8), X), rem(y + rem(div(i, 2), 4), Y), z, rem(c + rem(i, 2), 2)))
        return carry

    lax.fori_loop(1, 32, hello_plane, 0)
    hello(device(x, y, rem(z + 1, Z), c))
    hello(device(x, y, rem(z + Z - 1, Z), c))

    @pl.when(jnp.logical_not(l1_self))
    def _():
        hello(l1_to)
        hello(l1_from)

    for j in range(1, 8):
        hello(w_to(j))
    for i in range(8):
        pl.when(jnp.logical_not((i // 4 == yodd) & ((i // 2) % 2 == odd) & (i % 2 == c) & w_self))(
            lambda i=i: hello(w_from(i))
        )
    pl.when(jnp.logical_not(w_self))(lambda: hello(w_to(0)))
    pl.semaphore_wait(
        bar,
        31 + 2 + 16 + 2 - 2 * l1_self.astype(jnp.int32) - 2 * w_self.astype(jnp.int32),
    )

    def send(src, dst, send_sem, recv_sem, target, own=None):
        copy = pltpu.make_async_remote_copy(
            src_ref=src, dst_ref=dst, send_sem=send_sem, recv_sem=recv_sem,
            device_id=target, device_id_type=MESH,
        )
        if own is None:
            copy.start()
            return copy.wait_send
        pl.when(own)(lambda: pltpu.make_async_copy(src, dst, recv_sem).start())
        pl.when(jnp.logical_not(own))(copy.start)
        return lambda: pl.when(jnp.logical_not(own))(copy.wait_send)

    drains = []
    for h in range(2):
        rows = pl.ds(h * HALF, HALF)
        drains.append(send(
            left.at[0, 0, rows], lbuf.at[home, c, rows], l1_s.at[h], l_r.at[h], l1_to, l1_self))
    for j in range(4):
        own = (r_owner if j == 0 else None)
        drains.append(send(
            right.at[0, 0, pl.ds(0, RA)], rbuf.at[xodd, term, pl.ds(0, RA)],
            ra1_s.at[j], ra_r.at[xodd, term], device(x, rem(y + j, Y), z, xpair), own))
        drains.append(send(
            right.at[0, 0, pl.ds(RA, RB)], rbuf.at[xodd, term, pl.ds(RA, RB)],
            rb1_s.at[j], rb1_r.at[xodd, c], device(rem(x + j, X), y, z, xpair), own))
    for j in (1, 7, 2, 6, 3, 5, 4, 0):
        col = rem(z + j, Z)
        rows = pl.ds(pl.multiple_of(c * HALF, HALF), HALF)
        drains.append(send(
            wave.at[rows, pl.ds(pl.multiple_of((y * Z + col) * SEC, SEC), SEC)],
            wbuf.at[odd, yodd, rows], w_s.at[j], w_r.at[odd, yodd, c], w_to(j),
            w_self if j == 0 else None))

    acc[...] = jnp.zeros_like(acc)

    def ring(zh, rows, later, up):
        target = device(x, y, rem(z + jnp.where(up, 1, Z - 1), Z), c)
        send(lbuf.at[zh, c, rows], lbuf.at[zh, c, rows], ring_s.at[later], l_r.at[later], target)

    def to_sibling(n, zh, rows):
        send(lbuf.at[zh, c, rows], lbuf.at[zh, c, rows], sib_s.at[n], sib_r.at[n], sibling)

    for n, first, second in ((0, 2, 5), (1, 4, 3)):
        rows = pl.ds(n * HALF, HALF)
        received(lbuf.at[z, c, rows], l_r.at[n])
        ring(z, rows, first, True)
        ring(z, rows, second, False)
        to_sibling(n, z, rows)

    for s in range(2):
        for i in range(2):
            received(rbuf.at[s, 2 * y + i, pl.ds(RA, RB)], rb1_r.at[s, i])
    own_k = pl.ds(2 * y, 2)
    for j in range(1, 4):
        part = rbuf.at[:, own_k, pl.ds(RA, RB)]
        drains.append(send(part, part, rb2_s.at[j], rb2_r.at[j], device(x, rem(y + j, Y), z, c)))

    @pl.when(r_owner)
    def _():
        def forward(k, carry):
            part = rbuf.at[xodd, k, pl.ds(0, RA)]
            received(part, ra_r.at[xodd, k])
            for j in range(1, 4):
                send(part, part, ra2_s.at[j, k], ra_r.at[xodd, k], device(rem(x + j, X), y, z, c))
            return carry
        lax.fori_loop(0, 8, forward, 0)

    def place(n):
        m = jnp.maximum(n - 2, 0)
        d, r = div(m, 4) + 1, rem(m, 4)
        first = n < 2
        up = rem(r, 2) == 0
        h = jnp.where(first, n, ((r == 1) | (r == 2)).astype(jnp.int32))
        zh = jnp.where(first, z, rem(z + jnp.where(up, Z - d, d), Z))
        return zh, h, up

    def arrive(n):
        zh, h, up = place(n)
        rows = pl.ds(pl.multiple_of(h * HALF, HALF), HALF)
        received(lbuf.at[zh, c, rows], l_r.at[n])
        pl.when(n + 4 < CHUNKS)(lambda: ring(zh, rows, n + 4, up))
        to_sibling(n, zh, rows)

    def compute(n):
        zh, h, _ = place(n)
        rows = pl.ds(pl.multiple_of(h * HALF, HALF), HALF)
        received(lbuf.at[zh, 1 - c, rows], sib_r.at[n])
        e = rem(zh, 2)
        block = lbuf[zh, :, rows, :].reshape(2 * HALF, SEC)
        mid = dot3(split(block), (wh[e], wl[e]), ((1,), (0,)))
        for s in range(2):
            total = acc[s, e, rows, :]
            for core in range(2):
                k = 2 * term_pair(zh, core) + core
                part = split(mid[core * HALF:(core + 1) * HALF, s * SEC:(s + 1) * SEC])
                total += dot3(part, (rh[s, k], rl[s, k]), ((1,), (1,)))
            acc[s, e, rows, :] = total

    def step(n, carry):
        arrive(n)
        return carry

    lax.fori_loop(2, EARLY, step, 0)

    row_at = lax.broadcasted_iota(jnp.int32, (SEC, SEC), 0)
    col_at = lax.broadcasted_iota(jnp.int32, (SEC, SEC), 1)
    for e in range(2):
        for s in range(2):
            for i in range(2):
                received(wbuf.at[e, s, pl.ds(i * HALF, HALF)], w_r.at[e, s, i])
            inside = (row_at < ldims[x * Z + 2 * y + e]) & (col_at < rdims[(2 * c + s) * Z + z])
            high, low = split(jnp.where(inside, wbuf[e, s], 0.0))
            wh[e, :, s * SEC:(s + 1) * SEC] = high
            wl[e, :, s * SEC:(s + 1) * SEC] = low

    for j in range(1, 4):
        received(rbuf.at[:, pl.ds(2 * rem(y + Y - j, Y), 2), pl.ds(RA, RB)], rb2_r.at[j])
    for s in range(2):
        @pl.when(jnp.logical_not(r_owner & (xodd == s)))
        def _():
            def wait(k, carry):
                received(rbuf.at[s, k, pl.ds(0, RA)], ra_r.at[s, k])
                return carry
            lax.fori_loop(0, 8, wait, 0)

    def split_right(i, carry):
        s, k = div(i, 8), rem(i, 8)
        rh[s, k], rl[s, k] = split(rbuf[s, k])
        return carry

    lax.fori_loop(0, 16, split_right, 0)

    def both(n, carry):
        arrive(n)
        compute(n - LAG)
        return carry

    def late(n, carry):
        compute(n)
        return carry

    lax.fori_loop(EARLY, CHUNKS, both, 0)
    lax.fori_loop(CHUNKS - LAG, CHUNKS, late, 0)

    for i in range(2):
        rows = pl.ds(pl.multiple_of(yodd * 2 * SEC, 2 * SEC), 2 * SEC)
        drains.append(send(
            acc.at[i].reshape(2 * SEC, SEC), out.at[rows], o_s.at[i], o_r.at[yodd],
            device(2 * c + i, x, z, ypair), (x == y) & (c == ypair) & (xodd == i)))
    for drain in drains:
        drain()

    def drain_ring(n, carry):
        part = lbuf.at[0, 0, pl.ds(0, HALF)]
        pl.when(n >= 2)(lambda: pltpu.make_async_copy(part, part, ring_s.at[n]).wait())
        pltpu.make_async_copy(part, part, sib_s.at[n]).wait()
        return carry

    lax.fori_loop(0, CHUNKS, drain_ring, 0)

    @pl.when(r_owner)
    def _():
        def drain_right(k, carry):
            part = rbuf.at[0, 0, pl.ds(0, RA)]
            for j in range(1, 4):
                pltpu.make_async_copy(part, part, ra2_s.at[j, k]).wait()
            return carry
        lax.fori_loop(0, 8, drain_right, 0)

    for j in range(2):
        received(out.at[pl.ds(j * 2 * SEC, 2 * SEC)], o_r.at[j])


def shards(wave, left_env, right_env, left_dims, right_dims):
    dma = pltpu.SemaphoreType.DMA
    vmem, smem, hbm = pltpu.VMEM, pltpu.SMEM, pl.ANY
    raw = pl.pallas_call(
        kernel,
        out_shape=jax.ShapeDtypeStruct((4 * SEC, SEC), F32),
        in_specs=[pl.BlockSpec(memory_space=smem)] * 2 + [pl.BlockSpec(memory_space=hbm)] * 3,
        out_specs=pl.BlockSpec(memory_space=hbm),
        scratch_shapes=[
            vmem((Z, 2, SEC, SEC), F32),
            vmem((2, 8, SEC, SEC), F32),
            vmem((2, 2, SEC, SEC), F32),
            vmem((2, SEC, 2 * SEC), BF16),
            vmem((2, SEC, 2 * SEC), BF16),
            vmem((2, 8, SEC, SEC), BF16),
            vmem((2, 8, SEC, SEC), BF16),
            vmem((2, 2, SEC, SEC), F32),
            dma((2,)), dma((CHUNKS,)), dma((CHUNKS,)), dma((CHUNKS,)), dma((CHUNKS,)),
            dma((4,)), dma((4, 8)), dma((2, 8)), dma((4,)), dma((2, 2)), dma((4,)), dma((4,)),
            dma((8,)), dma((2, 2, 2)), dma((2,)), dma((2,)),
        ],
        compiler_params=pltpu.CompilerParams(
            collective_id=0, has_side_effects=True, vmem_limit_bytes=40 * 2 ** 20),
        cost_estimate=pl.CostEstimate(
            flops=6 * 64 * SEC ** 3, bytes_accessed=4 * 2 ** 20, transcendentals=0),
        name="two_site",
    )(left_dims, right_dims, wave, left_env, right_env)
    blk, term = lax.axis_index("blk"), lax.axis_index("term")
    rows = lax.broadcasted_iota(jnp.int32, (4, SEC, SEC), 1)
    cols = lax.broadcasted_iota(jnp.int32, (4, SEC, SEC), 2)
    own = lax.dynamic_slice_in_dim(left_dims, term * 4, 4, 0)
    inside = (rows < own[:, None, None]) & (cols < right_dims[blk])
    return jnp.where(inside, raw.reshape(4, SEC, SEC), 0.0).reshape(4 * SEC, SEC)


def solution(mesh):
    placed = (P("blk", None), P("term", "blk", None, None), P("term", "blk", None, None), P(), P())
    return jax.shard_map(
        shards, mesh=mesh, in_specs=placed, out_specs=P("term", "blk"), check_vma=False
    )
```

```python
import jax
import jax.numpy as jnp
from jax import lax
from jax.experimental import pallas as pl
from jax.experimental.pallas import tpu as pltpu
from jax.sharding import PartitionSpec as P

X, Y, Z = 4, 4, 8
SEC = 256
HALF = SEC // 2
RA = 128
RB = SEC - RA
CHUNKS = 16
PIECE = SEC // 4
AT_ONCE = 4
AT_RING = 6
RATE = 3
RELAY = 9
READY = 14
F32, BF16 = jnp.float32, jnp.bfloat16
MESH = pl.DeviceIdType.MESH


def device(x, y, z, c):
    return {"blk": x * Z + z, "term": y * 2 + c}


def rem(a, n):
    return lax.rem(a, jnp.int32(n))


def div(a, n):
    return lax.div(a, jnp.int32(n))


def split(a):
    high = a.astype(BF16)
    return high, (a - high.astype(F32)).astype(BF16)


def dot3(a, b, dims):
    (ah, al), (bh, bl) = a, b
    left = jnp.concatenate([ah, ah, al], dims[0])
    right = jnp.concatenate([bh, bl, bh], dims[1])
    return lax.dot_general(left, right, (((dims[0],), (dims[1],)), ((), ())), preferred_element_type=F32)


def received(ref, sem):
    pltpu.make_async_copy(ref, ref, sem).wait()


def kernel(
    ldims, rdims, wave, left, right, out,
    lbuf, rbuf, wbuf, lh, ll, wh, wl, rh, rl, acc,
    l1_s, ring_s, sib_s, l_r, sib_r,
    ra1_s, ra2_s, ra3_s, ra_r, rb1_s, rb1_r, rb2_s, rb2_r,
    w_s, w_r, o_s, o_r,
):
    blk, term = lax.axis_index("blk"), lax.axis_index("term")
    x, z = div(blk, Z), rem(blk, Z)
    y, c = div(term, 2), rem(term, 2)
    zpair, odd = div(z, 2), rem(z, 2)
    xpair, xodd = div(x, 2), rem(x, 2)
    ypair, yodd = div(y, 2), rem(y, 2)
    sibling = device(x, y, z, 1 - c)
    r_owner = c == xpair

    home = rem(z + 2 * rem(y + 2 * odd + c, 4), Z)
    l1_self = (zpair == y) & (home == z)
    l1_to = device(x, zpair, home, c)

    def term_pair(zh, core):
        return rem(div(zh, 2) - y - 2 * rem(zh, 2) - core + 8, 4)

    l1_from = device(x, term_pair(z, c), 2 * y + odd, c)

    def w_to(j):
        return device(x, zpair, rem(z + j, Z), ypair)

    def w_from(i):
        return device(x, 2 * c + i // 4, 2 * y + (i // 2) % 2, i % 2)

    w_self = (zpair == y) & (ypair == c)

    bar = pltpu.get_barrier_semaphore()

    def hello(target):
        pl.semaphore_signal(bar, inc=1, device_id=target, device_id_type=MESH)

    def hello_plane(i, carry):
        hello(device(rem(x + div(i, 8), X), rem(y + rem(div(i, 2), 4), Y), z, rem(c + rem(i, 2), 2)))
        return carry

    lax.fori_loop(1, 32, hello_plane, 0)
    hello(device(x, y, rem(z + 1, Z), c))
    hello(device(x, y, rem(z + Z - 1, Z), c))

    @pl.when(jnp.logical_not(l1_self))
    def _():
        hello(l1_to)
        hello(l1_from)

    for j in range(1, 8):
        hello(w_to(j))
    for i in range(8):
        pl.when(jnp.logical_not((i // 4 == yodd) & ((i // 2) % 2 == odd) & (i % 2 == c) & w_self))(
            lambda i=i: hello(w_from(i))
        )
    pl.when(jnp.logical_not(w_self))(lambda: hello(w_to(0)))
    pl.semaphore_wait(
        bar,
        31 + 2 + 16 + 2 - 2 * l1_self.astype(jnp.int32) - 2 * w_self.astype(jnp.int32),
    )

    def send(src, dst, send_sem, recv_sem, target, own=None):
        copy = pltpu.make_async_remote_copy(
            src_ref=src, dst_ref=dst, send_sem=send_sem, recv_sem=recv_sem,
            device_id=target, device_id_type=MESH,
        )
        if own is None:
            copy.start()
            return copy.wait_send
        pl.when(own)(lambda: pltpu.make_async_copy(src, dst, recv_sem).start())
        pl.when(jnp.logical_not(own))(copy.start)
        return lambda: pl.when(jnp.logical_not(own))(copy.wait_send)

    drains = []
    for h in range(2):
        rows = pl.ds(h * HALF, HALF)
        drains.append(send(
            left.at[0, 0, rows], lbuf.at[home, c, rows], l1_s.at[h], l_r.at[h], l1_to, l1_self))
    for j in range(4):
        own = (r_owner if j == 0 else None)
        drains.append(send(
            right.at[0, 0, pl.ds(0, RA)], rbuf.at[xodd, term, pl.ds(0, RA)],
            ra1_s.at[j], ra_r.at[xodd, term], device(x, rem(y + j, Y), z, xpair), own))
        drains.append(send(
            right.at[0, 0, pl.ds(RA, RB)], rbuf.at[xodd, term, pl.ds(RA, RB)],
            rb1_s.at[j], rb1_r.at[xodd, c], device(rem(x + j, X), y, z, xpair), own))
    quarter = 2 * yodd + c
    quarter_rows = pl.ds(pl.multiple_of(quarter * PIECE, PIECE), PIECE)

    def spread(i, carry):
        p, i = div(i, 8), rem(i, 8)
        j = jnp.where(i == 7, 0, jnp.where(rem(i, 2) == 0, div(i, 2) + 1, 7 - div(i, 2)))
        col = (2 * ypair + p) * Z + rem(z + j, Z)
        send(
            wave.at[quarter_rows, pl.ds(pl.multiple_of(col * SEC, SEC), SEC)],
            wbuf.at[odd, p, quarter_rows], w_s.at[p, i], w_r.at[p, odd, quarter], w_to(j),
            w_self & (i == 7))
        return carry

    lax.fori_loop(0, AT_ONCE, spread, 0)

    def ring(zh, rows, later, up):
        target = device(x, y, rem(z + jnp.where(up, 1, Z - 1), Z), c)
        send(lbuf.at[zh, c, rows], lbuf.at[zh, c, rows], ring_s.at[later], l_r.at[later], target)

    def to_sibling(n, zh, rows):
        send(lbuf.at[zh, c, rows], lbuf.at[zh, c, rows], sib_s.at[n], sib_r.at[n], sibling)

    for n, first, second in ((0, 2, 5), (1, 4, 3)):
        rows = pl.ds(n * HALF, HALF)
        received(lbuf.at[z, c, rows], l_r.at[n])
        ring(z, rows, first, True)
        ring(z, rows, second, False)
        to_sibling(n, z, rows)

    lax.fori_loop(AT_ONCE, AT_RING, spread, 0)

    for s in range(2):
        for i in range(2):
            received(rbuf.at[s, 2 * y + i, pl.ds(RA, RB)], rb1_r.at[s, i])

    def lower(yk, s):
        return rbuf.at[s, pl.ds(2 * yk, 2), pl.ds(RA, RB)]

    def upper(s, k):
        return rbuf.at[s, k, pl.ds(0, RA)]

    up_y, down_y = rem(y + 1, Y), rem(y + Y - 1, Y)
    up_x, down_x = rem(x + 1, X), rem(x + X - 1, X)
    for s in range(2):
        for way, to in enumerate((up_y, down_y)):
            drains.append(send(lower(y, s), lower(y, s), rb2_s.at[way, s], rb2_r.at[way, s], device(x, to, z, c)))

    @pl.when(r_owner)
    def _():
        def forward(k, carry):
            received(upper(xodd, k), ra_r.at[xodd, k])
            for way, to in enumerate((up_x, down_x)):
                send(upper(xodd, k), upper(xodd, k), ra2_s.at[way, k], ra_r.at[xodd, k], device(to, y, z, c))
            return carry
        lax.fori_loop(0, 8, forward, 0)

    def distance(s):
        return rem(x - (2 * c + s) + X, X)

    def relay():
        received(lower(down_y, 0), rb2_r.at[0, 0])
        drains.append(send(
            lower(down_y, 0), lower(down_y, 0), rb2_s.at[2, 0], rb2_r.at[2, 0], device(x, up_y, z, c)))
        received(lower(up_y, 1), rb2_r.at[1, 1])
        drains.append(send(
            lower(up_y, 1), lower(up_y, 1), rb2_s.at[2, 1], rb2_r.at[2, 1], device(x, down_y, z, c)))
        for s in range(2):
            for d, first, to in ((1, 0, up_x), (3, 1, down_x)):
                @pl.when(distance(s) == d)
                def _():
                    def forward(i, carry):
                        k = 2 * i + first
                        received(upper(s, k), ra_r.at[s, k])
                        send(upper(s, k), upper(s, k), ra3_s.at[s, k], ra_r.at[s, k], device(to, y, z, c))
                        return carry
                    lax.fori_loop(0, 4, forward, 0)

    def place(n):
        m = jnp.maximum(n - 2, 0)
        d, r = div(m, 4) + 1, rem(m, 4)
        first = n < 2
        up = rem(r, 2) == 0
        h = jnp.where(first, n, ((r == 1) | (r == 2)).astype(jnp.int32))
        zh = jnp.where(first, z, rem(z + jnp.where(up, Z - d, d), Z))
        return zh, h, up

    def arrive(n):
        zh, h, up = place(n)
        rows = pl.ds(pl.multiple_of(h * HALF, HALF), HALF)
        received(lbuf.at[zh, c, rows], l_r.at[n])
        pl.when(n + 4 < CHUNKS)(lambda: ring(zh, rows, n + 4, up))
        to_sibling(n, zh, rows)

    def prepare(n):
        zh, h, _ = place(n)
        rows = pl.ds(pl.multiple_of(h * HALF, HALF), HALF)
        received(lbuf.at[zh, 1 - c, rows], sib_r.at[n])
        lh[zh, :, rows, :], ll[zh, :, rows, :] = split(lbuf[zh, :, rows, :])

    def issued(n):
        return jnp.minimum(16, AT_RING + div((n - 1) * RATE, 4))

    def step(n, carry):
        arrive(n)
        lax.fori_loop(issued(n - 1), issued(n), spread, 0)
        prepare(n - 2)
        return carry

    def wait_right():
        received(lower(down_y, 1), rb2_r.at[0, 1])
        received(lower(up_y, 0), rb2_r.at[1, 0])
        for s in range(2):
            received(lower(rem(y + 2, Y), s), rb2_r.at[2, s])

            def wait(k, carry):
                d = distance(s)
                done = (d == 0) | ((d == 1) & (rem(k, 2) == 0)) | ((d == 3) & (rem(k, 2) == 1))
                pl.when(jnp.logical_not(done))(lambda: received(upper(s, k), ra_r.at[s, k]))
                return carry
            lax.fori_loop(0, 8, wait, 0)

    def split_right(i, carry):
        s, k = div(i, 8), rem(i, 8)
        rh[s, k], rl[s, k] = split(rbuf[s, k])
        return carry

    def ready():
        wait_right()
        lax.fori_loop(0, 16, split_right, 0)

    lax.fori_loop(2, RELAY, step, 0)
    relay()
    lax.fori_loop(RELAY, READY, step, 0)
    ready()
    lax.fori_loop(READY, CHUNKS, step, 0)
    lax.fori_loop(issued(CHUNKS - 1), 16, spread, 0)
    prepare(CHUNKS - 2)
    prepare(CHUNKS - 1)

    row_at = lax.broadcasted_iota(jnp.int32, (SEC, SEC), 0)
    col_at = lax.broadcasted_iota(jnp.int32, (SEC, SEC), 1)

    def product(s, e, m):
        zh = 2 * m + e
        flat = (2 * SEC, SEC)
        mid = dot3((lh[zh].reshape(flat), ll[zh].reshape(flat)), (wh[...], wl[...]), (1, 0))
        high, low = split(mid)
        parts = []
        for core in range(2):
            k = 2 * term_pair(zh, core) + core
            rows = slice(core * SEC, (core + 1) * SEC)
            parts.append((high[rows], low[rows], rh[s, k], rl[s, k]))
        (h0, l0, rh0, rl0), (h1, l1, rh1, rl1) = parts
        return dot3(
            (jnp.concatenate([h0, h1], 1), jnp.concatenate([l0, l1], 1)),
            (jnp.concatenate([rh0, rh1], 1), jnp.concatenate([rl0, rl1], 1)), (1, 1))

    for s in range(2):
        for e in range(2):
            inside = (row_at < ldims[x * Z + 2 * y + e]) & (col_at < rdims[(2 * c + s) * Z + z])
            for q in range(4):
                received(wbuf.at[e, s, pl.ds(q * PIECE, PIECE)], w_r.at[s, e, q])
            wh[...], wl[...] = split(jnp.where(inside, wbuf[e, s], 0.0))
            acc[s, e] = product(s, e, 0)
            for m in range(1, 4):
                acc[s, e] += product(s, e, m)
            acc[s, e] = jnp.where(inside, acc[s, e], 0.0)
            send(
                acc.at[s, e], out.at[2 * yodd + e], o_s.at[s, e], o_r.at[2 * yodd + e],
                device(2 * c + s, x, z, ypair), (x == y) & (c == ypair) & (xodd == s))

    for drain in drains:
        drain()
    for s in range(2):
        @pl.when(jnp.logical_not((x == y) & (c == ypair) & (xodd == s)))
        def _():
            for e in range(2):
                received(acc.at[s, e], o_s.at[s, e])

    def drain_wave(i, carry):
        part = wbuf.at[0, 0, pl.ds(0, PIECE)]
        pl.when(jnp.logical_not(w_self & (rem(i, 8) == 7)))(
            lambda: received(part, w_s.at[div(i, 8), rem(i, 8)]))
        return carry

    lax.fori_loop(0, 16, drain_wave, 0)

    def drain_ring(n, carry):
        part = lbuf.at[0, 0, pl.ds(0, HALF)]
        pl.when(n >= 2)(lambda: pltpu.make_async_copy(part, part, ring_s.at[n]).wait())
        pltpu.make_async_copy(part, part, sib_s.at[n]).wait()
        return carry

    lax.fori_loop(0, CHUNKS, drain_ring, 0)

    @pl.when(r_owner)
    def _():
        def drain_right(k, carry):
            for way in range(2):
                received(upper(0, 0), ra2_s.at[way, k])
            return carry
        lax.fori_loop(0, 8, drain_right, 0)

    for s in range(2):
        for d, first in ((1, 0), (3, 1)):
            @pl.when(distance(s) == d)
            def _():
                def drain_relay(i, carry):
                    received(upper(0, 0), ra3_s.at[s, 2 * i + first])
                    return carry
                lax.fori_loop(0, 4, drain_relay, 0)

    for j in range(4):
        received(out.at[j], o_r.at[j])


def shards(wave, left_env, right_env, left_dims, right_dims):
    dma = pltpu.SemaphoreType.DMA
    vmem, smem, hbm = pltpu.VMEM, pltpu.SMEM, pl.ANY
    return pl.pallas_call(
        kernel,
        out_shape=jax.ShapeDtypeStruct((4, SEC, SEC), F32),
        in_specs=[pl.BlockSpec(memory_space=smem)] * 2 + [pl.BlockSpec(memory_space=hbm)] * 3,
        out_specs=pl.BlockSpec(memory_space=vmem),
        scratch_shapes=[
            vmem((Z, 2, SEC, SEC), F32),
            vmem((2, 8, SEC, SEC), F32),
            vmem((2, 2, SEC, SEC), F32),
            vmem((Z, 2, SEC, SEC), BF16),
            vmem((Z, 2, SEC, SEC), BF16),
            vmem((SEC, SEC), BF16),
            vmem((SEC, SEC), BF16),
            vmem((2, 8, SEC, SEC), BF16),
            vmem((2, 8, SEC, SEC), BF16),
            vmem((2, 2, SEC, SEC), F32),
            dma((2,)), dma((CHUNKS,)), dma((CHUNKS,)), dma((CHUNKS,)), dma((CHUNKS,)),
            dma((4,)), dma((2, 8)), dma((2, 8)), dma((2, 8)), dma((4,)), dma((2, 2)), dma((3, 2)), dma((3, 2)),
            dma((2, 8)), dma((2, 2, 4)), dma((2, 2)), dma((4,)),
        ],
        compiler_params=pltpu.CompilerParams(
            collective_id=0, has_side_effects=True, vmem_limit_bytes=60 * 2 ** 20),
        cost_estimate=pl.CostEstimate(
            flops=6 * 64 * SEC ** 3, bytes_accessed=4 * 2 ** 20, transcendentals=0),
        name="two_site",
    )(left_dims, right_dims, wave, left_env, right_env).reshape(4 * SEC, SEC)


def solution(mesh):
    placed = (P("blk", None), P("term", "blk", None, None), P("term", "blk", None, None), P(), P())
    return jax.shard_map(
        shards, mesh=mesh, in_specs=placed, out_specs=P("term", "blk"), check_vma=False
    )
```

```python
import jax
import jax.numpy as jnp
from jax import lax
from jax.experimental import pallas as pl
from jax.experimental.pallas import tpu as pltpu
from jax.sharding import PartitionSpec as P

X, Y, Z = 4, 4, 8
SEC = 256
HALF = SEC // 2
RA = 128
RB = SEC - RA
CHUNKS = 16
PIECE = SEC // 4
AT_ONCE = 4
AT_RING = 6
RATE = 3
RELAY = 9
READY = 14
F32, BF16 = jnp.float32, jnp.bfloat16
MESH = pl.DeviceIdType.MESH


def device(x, y, z, c):
    return {"blk": x * Z + z, "term": y * 2 + c}


def rem(a, n):
    return lax.rem(a, jnp.int32(n))


def div(a, n):
    return lax.div(a, jnp.int32(n))


def split(a):
    high = a.astype(BF16)
    return high, (a - high.astype(F32)).astype(BF16)


def dot3(a, b, dims):
    (ah, al), (bh, bl) = a, b
    left = jnp.concatenate([ah, ah, al], dims[0])
    right = jnp.concatenate([bh, bl, bh], dims[1])
    return lax.dot_general(left, right, (((dims[0],), (dims[1],)), ((), ())), preferred_element_type=F32)


def received(ref, sem):
    pltpu.make_async_copy(ref, ref, sem).wait()


def kernel(
    ldims, rdims, wave, left, right, out,
    lbuf, rbuf, wbuf, lh, ll, wh, wl, rh, rl, acc,
    l1_s, ring_s, sib_s, l_r, sib_r,
    ra1_s, ra2_s, ra3_s, ra_r, rb1_s, rb1_r, rb2_s, rb2_r,
    w_s, w_r, o_s, o_r,
):
    blk, term = lax.axis_index("blk"), lax.axis_index("term")
    x, z = div(blk, Z), rem(blk, Z)
    y, c = div(term, 2), rem(term, 2)
    zpair, odd = div(z, 2), rem(z, 2)
    xpair, xodd = div(x, 2), rem(x, 2)
    ypair, yodd = div(y, 2), rem(y, 2)
    sibling = device(x, y, z, 1 - c)
    r_owner = c == xpair

    home = rem(z + 2 * rem(y + 2 * odd + c, 4), Z)
    l1_self = (zpair == y) & (home == z)
    l1_to = device(x, zpair, home, c)

    def term_pair(zh, core):
        return rem(div(zh, 2) - y - 2 * rem(zh, 2) - core + 8, 4)

    l1_from = device(x, term_pair(z, c), 2 * y + odd, c)

    def w_to(j):
        return device(x, zpair, rem(z + j, Z), ypair)

    def w_from(i):
        return device(x, 2 * c + i // 4, 2 * y + (i // 2) % 2, i % 2)

    w_self = (zpair == y) & (ypair == c)

    bar = pltpu.get_barrier_semaphore()

    def hello(target):
        pl.semaphore_signal(bar, inc=1, device_id=target, device_id_type=MESH)

    def hello_plane(i, carry):
        hello(device(rem(x + div(i, 8), X), rem(y + rem(div(i, 2), 4), Y), z, rem(c + rem(i, 2), 2)))
        return carry

    lax.fori_loop(1, 32, hello_plane, 0)
    hello(device(x, y, rem(z + 1, Z), c))
    hello(device(x, y, rem(z + Z - 1, Z), c))

    @pl.when(jnp.logical_not(l1_self))
    def _():
        hello(l1_to)
        hello(l1_from)

    for j in range(1, 8):
        hello(w_to(j))
    for i in range(8):
        pl.when(jnp.logical_not((i // 4 == yodd) & ((i // 2) % 2 == odd) & (i % 2 == c) & w_self))(
            lambda i=i: hello(w_from(i))
        )
    pl.when(jnp.logical_not(w_self))(lambda: hello(w_to(0)))
    pl.semaphore_wait(
        bar,
        31 + 2 + 16 + 2 - 2 * l1_self.astype(jnp.int32) - 2 * w_self.astype(jnp.int32),
    )

    def send(src, dst, send_sem, recv_sem, target, own=None):
        copy = pltpu.make_async_remote_copy(
            src_ref=src, dst_ref=dst, send_sem=send_sem, recv_sem=recv_sem,
            device_id=target, device_id_type=MESH,
        )
        if own is None:
            copy.start()
            return copy.wait_send
        pl.when(own)(lambda: pltpu.make_async_copy(src, dst, recv_sem).start())
        pl.when(jnp.logical_not(own))(copy.start)
        return lambda: pl.when(jnp.logical_not(own))(copy.wait_send)

    drains = []
    for h in range(2):
        rows = pl.ds(h * HALF, HALF)
        drains.append(send(
            left.at[0, 0, rows], lbuf.at[home, c, rows], l1_s.at[h], l_r.at[h], l1_to, l1_self))
    for j in range(4):
        own = (r_owner if j == 0 else None)
        drains.append(send(
            right.at[0, 0, pl.ds(0, RA)], rbuf.at[xodd, term, pl.ds(0, RA)],
            ra1_s.at[j], ra_r.at[xodd, term], device(x, rem(y + j, Y), z, xpair), own))
        drains.append(send(
            right.at[0, 0, pl.ds(RA, RB)], rbuf.at[xodd, term, pl.ds(RA, RB)],
            rb1_s.at[j], rb1_r.at[xodd, c], device(rem(x + j, X), y, z, xpair), own))
    quarter = 2 * yodd + c
    quarter_rows = pl.ds(pl.multiple_of(quarter * PIECE, PIECE), PIECE)

    def spread(i, carry):
        p, i = div(i, 8), rem(i, 8)
        j = jnp.where(i == 7, 0, jnp.where(rem(i, 2) == 0, div(i, 2) + 1, 7 - div(i, 2)))
        col = (2 * ypair + p) * Z + rem(z + j, Z)
        send(
            wave.at[quarter_rows, pl.ds(pl.multiple_of(col * SEC, SEC), SEC)],
            wbuf.at[odd, p, quarter_rows], w_s.at[p, i], w_r.at[p, odd, quarter], w_to(j),
            w_self & (i == 7))
        return carry

    lax.fori_loop(0, AT_ONCE, spread, 0)

    def ring(zh, rows, later, up):
        target = device(x, y, rem(z + jnp.where(up, 1, Z - 1), Z), c)
        send(lbuf.at[zh, c, rows], lbuf.at[zh, c, rows], ring_s.at[later], l_r.at[later], target)

    def to_sibling(n, zh, rows):
        send(lbuf.at[zh, c, rows], lbuf.at[zh, c, rows], sib_s.at[n], sib_r.at[n], sibling)

    for n, first, second in ((0, 2, 5), (1, 4, 3)):
        rows = pl.ds(n * HALF, HALF)
        received(lbuf.at[z, c, rows], l_r.at[n])
        ring(z, rows, first, True)
        ring(z, rows, second, False)
        to_sibling(n, z, rows)

    lax.fori_loop(AT_ONCE, AT_RING, spread, 0)

    for s in range(2):
        for i in range(2):
            received(rbuf.at[s, 2 * y + i, pl.ds(RA, RB)], rb1_r.at[s, i])

    def lower(yk, s):
        return rbuf.at[s, pl.ds(2 * yk, 2), pl.ds(RA, RB)]

    def upper(s, k):
        return rbuf.at[s, k, pl.ds(0, RA)]

    up_y, down_y = rem(y + 1, Y), rem(y + Y - 1, Y)
    up_x, down_x = rem(x + 1, X), rem(x + X - 1, X)
    for s in range(2):
        for way, to in enumerate((up_y, down_y)):
            drains.append(send(lower(y, s), lower(y, s), rb2_s.at[way, s], rb2_r.at[way, s], device(x, to, z, c)))

    @pl.when(r_owner)
    def _():
        def forward(k, carry):
            received(upper(xodd, k), ra_r.at[xodd, k])
            for way, to in enumerate((up_x, down_x)):
                send(upper(xodd, k), upper(xodd, k), ra2_s.at[way, k], ra_r.at[xodd, k], device(to, y, z, c))
            return carry
        lax.fori_loop(0, 8, forward, 0)

    def distance(s):
        return rem(x - (2 * c + s) + X, X)

    def relay():
        received(lower(down_y, 0), rb2_r.at[0, 0])
        drains.append(send(
            lower(down_y, 0), lower(down_y, 0), rb2_s.at[2, 0], rb2_r.at[2, 0], device(x, up_y, z, c)))
        received(lower(up_y, 1), rb2_r.at[1, 1])
        drains.append(send(
            lower(up_y, 1), lower(up_y, 1), rb2_s.at[2, 1], rb2_r.at[2, 1], device(x, down_y, z, c)))
        for s in range(2):
            for d, first, to in ((1, 0, up_x), (3, 1, down_x)):
                @pl.when(distance(s) == d)
                def _():
                    def forward(i, carry):
                        k = 2 * i + first
                        received(upper(s, k), ra_r.at[s, k])
                        send(upper(s, k), upper(s, k), ra3_s.at[s, k], ra_r.at[s, k], device(to, y, z, c))
                        return carry
                    lax.fori_loop(0, 4, forward, 0)

    def place(n):
        m = jnp.maximum(n - 2, 0)
        d, r = div(m, 4) + 1, rem(m, 4)
        first = n < 2
        up = rem(r, 2) == 0
        h = jnp.where(first, n, ((r == 1) | (r == 2)).astype(jnp.int32))
        zh = jnp.where(first, z, rem(z + jnp.where(up, Z - d, d), Z))
        return zh, h, up

    def arrive(n):
        zh, h, up = place(n)
        rows = pl.ds(pl.multiple_of(h * HALF, HALF), HALF)
        received(lbuf.at[zh, c, rows], l_r.at[n])
        pl.when(n + 4 < CHUNKS)(lambda: ring(zh, rows, n + 4, up))
        to_sibling(n, zh, rows)

    def prepare(n):
        zh, h, _ = place(n)
        rows = pl.ds(pl.multiple_of(h * HALF, HALF), HALF)
        received(lbuf.at[zh, 1 - c, rows], sib_r.at[n])
        lh[zh, :, rows, :], ll[zh, :, rows, :] = split(lbuf[zh, :, rows, :])

    def issued(n):
        return jnp.minimum(16, AT_RING + div((n - 1) * RATE, 4))

    def step(n, carry):
        arrive(n)
        lax.fori_loop(issued(n - 1), issued(n), spread, 0)
        prepare(n - 2)
        return carry

    def wait_right():
        received(lower(down_y, 1), rb2_r.at[0, 1])
        received(lower(up_y, 0), rb2_r.at[1, 0])
        for s in range(2):
            received(lower(rem(y + 2, Y), s), rb2_r.at[2, s])

            def wait(k, carry):
                d = distance(s)
                done = (d == 0) | ((d == 1) & (rem(k, 2) == 0)) | ((d == 3) & (rem(k, 2) == 1))
                pl.when(jnp.logical_not(done))(lambda: received(upper(s, k), ra_r.at[s, k]))
                return carry
            lax.fori_loop(0, 8, wait, 0)

    def split_right(i, carry):
        s, k = div(i, 8), rem(i, 8)
        rh[s, k], rl[s, k] = split(rbuf[s, k])
        return carry

    def ready():
        wait_right()
        lax.fori_loop(0, 16, split_right, 0)

    lax.fori_loop(2, RELAY, step, 0)
    relay()
    lax.fori_loop(RELAY, READY, step, 0)
    ready()
    lax.fori_loop(READY, CHUNKS - 2, step, 0)
    prepare(CHUNKS - 4)
    prepare(CHUNKS - 3)
    lax.fori_loop(issued(CHUNKS - 3), issued(CHUNKS - 1), spread, 0)

    row_at = lax.broadcasted_iota(jnp.int32, (SEC, SEC), 0)
    col_at = lax.broadcasted_iota(jnp.int32, (SEC, SEC), 1)

    def product(s, e, m):
        zh = 2 * m + e
        flat = (2 * SEC, SEC)
        mid = dot3((lh[zh].reshape(flat), ll[zh].reshape(flat)), (wh[...], wl[...]), (1, 0))
        high, low = split(mid)
        parts = []
        for core in range(2):
            k = 2 * term_pair(zh, core) + core
            rows = slice(core * SEC, (core + 1) * SEC)
            parts.append((high[rows], low[rows], rh[s, k], rl[s, k]))
        (h0, l0, rh0, rl0), (h1, l1, rh1, rl1) = parts
        return dot3(
            (jnp.concatenate([h0, h1], 1), jnp.concatenate([l0, l1], 1)),
            (jnp.concatenate([rh0, rh1], 1), jnp.concatenate([rl0, rl1], 1)), (1, 1))

    for s in range(2):
        for e in (1 - odd, odd):
            inside = (row_at < ldims[x * Z + 2 * y + e]) & (col_at < rdims[(2 * c + s) * Z + z])
            for q in range(4):
                received(wbuf.at[e, s, pl.ds(q * PIECE, PIECE)], w_r.at[s, e, q])
            wh[...], wl[...] = split(jnp.where(inside, wbuf[e, s], 0.0))
            acc[s, e] = product(s, e, 0)
            for m in range(1, 4):
                acc[s, e] += product(s, e, m)
            acc[s, e] = jnp.where(inside, acc[s, e], 0.0)
            send(
                acc.at[s, e], out.at[2 * yodd + e], o_s.at[s, e], o_r.at[2 * yodd + e],
                device(2 * c + s, x, z, ypair), (x == y) & (c == ypair) & (xodd == s))
            if s == 0 and e is not odd:
                for n in (CHUNKS - 2, CHUNKS - 1):
                    arrive(n)
                lax.fori_loop(issued(CHUNKS - 1), 16, spread, 0)
                for n in (CHUNKS - 2, CHUNKS - 1):
                    prepare(n)

    for drain in drains:
        drain()
    for s in range(2):
        @pl.when(jnp.logical_not((x == y) & (c == ypair) & (xodd == s)))
        def _():
            for e in range(2):
                received(acc.at[s, e], o_s.at[s, e])

    def drain_wave(i, carry):
        part = wbuf.at[0, 0, pl.ds(0, PIECE)]
        pl.when(jnp.logical_not(w_self & (rem(i, 8) == 7)))(
            lambda: received(part, w_s.at[div(i, 8), rem(i, 8)]))
        return carry

    lax.fori_loop(0, 16, drain_wave, 0)

    def drain_ring(n, carry):
        part = lbuf.at[0, 0, pl.ds(0, HALF)]
        pl.when(n >= 2)(lambda: pltpu.make_async_copy(part, part, ring_s.at[n]).wait())
        pltpu.make_async_copy(part, part, sib_s.at[n]).wait()
        return carry

    lax.fori_loop(0, CHUNKS, drain_ring, 0)

    @pl.when(r_owner)
    def _():
        def drain_right(k, carry):
            for way in range(2):
                received(upper(0, 0), ra2_s.at[way, k])
            return carry
        lax.fori_loop(0, 8, drain_right, 0)

    for s in range(2):
        for d, first in ((1, 0), (3, 1)):
            @pl.when(distance(s) == d)
            def _():
                def drain_relay(i, carry):
                    received(upper(0, 0), ra3_s.at[s, 2 * i + first])
                    return carry
                lax.fori_loop(0, 4, drain_relay, 0)

    for j in range(4):
        received(out.at[j], o_r.at[j])


def shards(wave, left_env, right_env, left_dims, right_dims):
    dma = pltpu.SemaphoreType.DMA
    vmem, smem, hbm = pltpu.VMEM, pltpu.SMEM, pl.ANY
    return pl.pallas_call(
        kernel,
        out_shape=jax.ShapeDtypeStruct((4, SEC, SEC), F32),
        in_specs=[pl.BlockSpec(memory_space=smem)] * 2 + [pl.BlockSpec(memory_space=hbm)] * 3,
        out_specs=pl.BlockSpec(memory_space=hbm),
        scratch_shapes=[
            vmem((Z, 2, SEC, SEC), F32),
            vmem((2, 8, SEC, SEC), F32),
            vmem((2, 2, SEC, SEC), F32),
            vmem((Z, 2, SEC, SEC), BF16),
            vmem((Z, 2, SEC, SEC), BF16),
            vmem((SEC, SEC), BF16),
            vmem((SEC, SEC), BF16),
            vmem((2, 8, SEC, SEC), BF16),
            vmem((2, 8, SEC, SEC), BF16),
            vmem((2, 2, SEC, SEC), F32),
            dma((2,)), dma((CHUNKS,)), dma((CHUNKS,)), dma((CHUNKS,)), dma((CHUNKS,)),
            dma((4,)), dma((2, 8)), dma((2, 8)), dma((2, 8)), dma((4,)), dma((2, 2)), dma((3, 2)), dma((3, 2)),
            dma((2, 8)), dma((2, 2, 4)), dma((2, 2)), dma((4,)),
        ],
        compiler_params=pltpu.CompilerParams(
            collective_id=0, has_side_effects=True, vmem_limit_bytes=60 * 2 ** 20),
        cost_estimate=pl.CostEstimate(
            flops=6 * 64 * SEC ** 3, bytes_accessed=4 * 2 ** 20, transcendentals=0),
        name="two_site",
    )(left_dims, right_dims, wave, left_env, right_env).reshape(4 * SEC, SEC)


def solution(mesh):
    placed = (P("blk", None), P("term", "blk", None, None), P("term", "blk", None, None), P(), P())
    return jax.shard_map(
        shards, mesh=mesh, in_specs=placed, out_specs=P("term", "blk"), check_vma=False
    )
```

```python
import jax
import jax.numpy as jnp
from jax import lax
from jax.experimental import pallas as pl
from jax.experimental.pallas import tpu as pltpu
from jax.sharding import PartitionSpec as P

X, Y, Z = 4, 4, 8
SEC = 256
HALF = SEC // 2
RA = 128
RB = SEC - RA
CHUNKS = 16
PIECE = SEC // 4
AT_ONCE = 4
AT_RING = 6
RATE = 3
RELAY = 9
READY = 14
F32, BF16 = jnp.float32, jnp.bfloat16
MESH = pl.DeviceIdType.MESH


def device(x, y, z, c):
    return {"blk": x * Z + z, "term": y * 2 + c}


def rem(a, n):
    return lax.rem(a, jnp.int32(n))


def div(a, n):
    return lax.div(a, jnp.int32(n))


def split(a):
    high = a.astype(BF16)
    return high, (a - high.astype(F32)).astype(BF16)


def dot3(a, b, dims):
    (ah, al), (bh, bl) = a, b
    left = jnp.concatenate([ah, ah, al], dims[0])
    right = jnp.concatenate([bh, bl, bh], dims[1])
    return lax.dot_general(left, right, (((dims[0],), (dims[1],)), ((), ())), preferred_element_type=F32)


def received(ref, sem):
    pltpu.make_async_copy(ref, ref, sem).wait()


def kernel(
    ldims, rdims, wave, left, right, out,
    lbuf, rbuf, wbuf, lh, ll, wh, wl, rh, rl, acc,
    l1_s, ring_s, sib_s, l_r, sib_r,
    ra1_s, ra2_s, ra3_s, ra_r, rb1_s, rb1_r, rb2_s, rb2_r,
    w_s, w_r, o_s, o_r,
):
    blk, term = lax.axis_index("blk"), lax.axis_index("term")
    x, z = div(blk, Z), rem(blk, Z)
    y, c = div(term, 2), rem(term, 2)
    zpair, odd = div(z, 2), rem(z, 2)
    xpair, xodd = div(x, 2), rem(x, 2)
    ypair, yodd = div(y, 2), rem(y, 2)
    sibling = device(x, y, z, 1 - c)
    r_owner = c == xpair

    home = rem(z + 2 * rem(y + 2 * odd + c, 4), Z)
    l1_self = (zpair == y) & (home == z)
    l1_to = device(x, zpair, home, c)

    def term_pair(zh, core):
        return rem(div(zh, 2) - y - 2 * rem(zh, 2) - core + 8, 4)

    l1_from = device(x, term_pair(z, c), 2 * y + odd, c)

    def w_to(j):
        return device(x, zpair, rem(z + j, Z), ypair)

    def w_from(i):
        return device(x, 2 * c + i // 4, 2 * y + (i // 2) % 2, i % 2)

    w_self = (zpair == y) & (ypair == c)

    bar = pltpu.get_barrier_semaphore()

    def hello(target):
        pl.semaphore_signal(bar, inc=1, device_id=target, device_id_type=MESH)

    def hello_plane(i, carry):
        hello(device(rem(x + div(i, 8), X), rem(y + rem(div(i, 2), 4), Y), z, rem(c + rem(i, 2), 2)))
        return carry

    lax.fori_loop(1, 32, hello_plane, 0)
    hello(device(x, y, rem(z + 1, Z), c))
    hello(device(x, y, rem(z + Z - 1, Z), c))

    @pl.when(jnp.logical_not(l1_self))
    def _():
        hello(l1_to)
        hello(l1_from)

    for j in range(1, 8):
        hello(w_to(j))
    for i in range(8):
        pl.when(jnp.logical_not((i // 4 == yodd) & ((i // 2) % 2 == odd) & (i % 2 == c) & w_self))(
            lambda i=i: hello(w_from(i))
        )
    pl.when(jnp.logical_not(w_self))(lambda: hello(w_to(0)))
    pl.semaphore_wait(
        bar,
        31 + 2 + 16 + 2 - 2 * l1_self.astype(jnp.int32) - 2 * w_self.astype(jnp.int32),
    )

    def send(src, dst, send_sem, recv_sem, target, own=None):
        copy = pltpu.make_async_remote_copy(
            src_ref=src, dst_ref=dst, send_sem=send_sem, recv_sem=recv_sem,
            device_id=target, device_id_type=MESH,
        )
        if own is None:
            copy.start()
            return copy.wait_send
        pl.when(own)(lambda: pltpu.make_async_copy(src, dst, recv_sem).start())
        pl.when(jnp.logical_not(own))(copy.start)
        return lambda: pl.when(jnp.logical_not(own))(copy.wait_send)

    drains = []
    for h in range(2):
        rows = pl.ds(h * HALF, HALF)
        drains.append(send(
            left.at[0, 0, rows], lbuf.at[home, c, rows], l1_s.at[h], l_r.at[h], l1_to, l1_self))
    for j in range(4):
        own = (r_owner if j == 0 else None)
        drains.append(send(
            right.at[0, 0, pl.ds(0, RA)], rbuf.at[xodd, term, pl.ds(0, RA)],
            ra1_s.at[j], ra_r.at[xodd, term], device(x, rem(y + j, Y), z, xpair), own))
        drains.append(send(
            right.at[0, 0, pl.ds(RA, RB)], rbuf.at[xodd, term, pl.ds(RA, RB)],
            rb1_s.at[j], rb1_r.at[xodd, c], device(rem(x + j, X), y, z, xpair), own))
    quarter = 2 * yodd + c
    quarter_rows = pl.ds(pl.multiple_of(quarter * PIECE, PIECE), PIECE)

    def spread(i, carry):
        p, i = div(i, 8), rem(i, 8)
        j = jnp.where(i == 7, 0, jnp.where(rem(i, 2) == 0, div(i, 2) + 1, 7 - div(i, 2)))
        s = rem(p + xodd, 2)
        col = (2 * ypair + s) * Z + rem(z + j, Z)
        send(
            wave.at[quarter_rows, pl.ds(pl.multiple_of(col * SEC, SEC), SEC)],
            wbuf.at[odd, s, quarter_rows], w_s.at[p, i], w_r.at[s, odd, quarter], w_to(j),
            w_self & (i == 7))
        return carry

    lax.fori_loop(0, AT_ONCE, spread, 0)

    def ring(zh, rows, later, up):
        target = device(x, y, rem(z + jnp.where(up, 1, Z - 1), Z), c)
        send(lbuf.at[zh, c, rows], lbuf.at[zh, c, rows], ring_s.at[later], l_r.at[later], target)

    def to_sibling(n, zh, rows):
        send(lbuf.at[zh, c, rows], lbuf.at[zh, c, rows], sib_s.at[n], sib_r.at[n], sibling)

    for n, first, second in ((0, 2, 5), (1, 4, 3)):
        rows = pl.ds(n * HALF, HALF)
        received(lbuf.at[z, c, rows], l_r.at[n])
        ring(z, rows, first, True)
        ring(z, rows, second, False)
        to_sibling(n, z, rows)

    lax.fori_loop(AT_ONCE, AT_RING, spread, 0)

    for s in range(2):
        for i in range(2):
            received(rbuf.at[s, 2 * y + i, pl.ds(RA, RB)], rb1_r.at[s, i])

    def lower(yk, s):
        return rbuf.at[s, pl.ds(2 * yk, 2), pl.ds(RA, RB)]

    def upper(s, k):
        return rbuf.at[s, k, pl.ds(0, RA)]

    up_y, down_y = rem(y + 1, Y), rem(y + Y - 1, Y)
    up_x, down_x = rem(x + 1, X), rem(x + X - 1, X)
    for s in range(2):
        for way, to in enumerate((up_y, down_y)):
            drains.append(send(lower(y, s), lower(y, s), rb2_s.at[way, s], rb2_r.at[way, s], device(x, to, z, c)))

    @pl.when(r_owner)
    def _():
        def forward(k, carry):
            received(upper(xodd, k), ra_r.at[xodd, k])
            for way, to in enumerate((up_x, down_x)):
                send(upper(xodd, k), upper(xodd, k), ra2_s.at[way, k], ra_r.at[xodd, k], device(to, y, z, c))
            return carry
        lax.fori_loop(0, 8, forward, 0)

    def distance(s):
        return rem(x - (2 * c + s) + X, X)

    def relay():
        received(lower(down_y, 0), rb2_r.at[0, 0])
        drains.append(send(
            lower(down_y, 0), lower(down_y, 0), rb2_s.at[2, 0], rb2_r.at[2, 0], device(x, up_y, z, c)))
        received(lower(up_y, 1), rb2_r.at[1, 1])
        drains.append(send(
            lower(up_y, 1), lower(up_y, 1), rb2_s.at[2, 1], rb2_r.at[2, 1], device(x, down_y, z, c)))
        for s in range(2):
            for d, first, to in ((1, 0, up_x), (3, 1, down_x)):
                @pl.when(distance(s) == d)
                def _():
                    def forward(i, carry):
                        k = 2 * i + first
                        received(upper(s, k), ra_r.at[s, k])
                        send(upper(s, k), upper(s, k), ra3_s.at[s, k], ra_r.at[s, k], device(to, y, z, c))
                        return carry
                    lax.fori_loop(0, 4, forward, 0)

    def place(n):
        m = jnp.maximum(n - 2, 0)
        d, r = div(m, 4) + 1, rem(m, 4)
        first = n < 2
        up = rem(r, 2) == 0
        h = jnp.where(first, n, ((r == 1) | (r == 2)).astype(jnp.int32))
        zh = jnp.where(first, z, rem(z + jnp.where(up, Z - d, d), Z))
        return zh, h, up

    def arrive(n):
        zh, h, up = place(n)
        rows = pl.ds(pl.multiple_of(h * HALF, HALF), HALF)
        received(lbuf.at[zh, c, rows], l_r.at[n])
        pl.when(n + 4 < CHUNKS)(lambda: ring(zh, rows, n + 4, up))
        to_sibling(n, zh, rows)

    def prepare(n):
        zh, h, _ = place(n)
        rows = pl.ds(pl.multiple_of(h * HALF, HALF), HALF)
        received(lbuf.at[zh, 1 - c, rows], sib_r.at[n])
        lh[zh, :, rows, :], ll[zh, :, rows, :] = split(lbuf[zh, :, rows, :])

    def issued(n):
        return jnp.minimum(16, AT_RING + div((n - 1) * RATE, 4))

    def step(n, carry):
        arrive(n)
        lax.fori_loop(issued(n - 1), issued(n), spread, 0)
        prepare(n - 2)
        return carry

    def wait_right():
        received(lower(down_y, 1), rb2_r.at[0, 1])
        received(lower(up_y, 0), rb2_r.at[1, 0])
        for s in range(2):
            received(lower(rem(y + 2, Y), s), rb2_r.at[2, s])

            def wait(k, carry):
                d = distance(s)
                done = (d == 0) | ((d == 1) & (rem(k, 2) == 0)) | ((d == 3) & (rem(k, 2) == 1))
                pl.when(jnp.logical_not(done))(lambda: received(upper(s, k), ra_r.at[s, k]))
                return carry
            lax.fori_loop(0, 8, wait, 0)

    def split_right(i, carry):
        s, k = div(i, 8), rem(i, 8)
        rh[s, k], rl[s, k] = split(rbuf[s, k])
        return carry

    def ready():
        wait_right()
        lax.fori_loop(0, 16, split_right, 0)

    lax.fori_loop(2, RELAY, step, 0)
    relay()
    lax.fori_loop(RELAY, READY, step, 0)
    ready()
    lax.fori_loop(READY, CHUNKS - 2, step, 0)
    prepare(CHUNKS - 4)
    prepare(CHUNKS - 3)
    lax.fori_loop(issued(CHUNKS - 3), issued(CHUNKS - 1), spread, 0)

    row_at = lax.broadcasted_iota(jnp.int32, (SEC, SEC), 0)
    col_at = lax.broadcasted_iota(jnp.int32, (SEC, SEC), 1)

    def product(s, e, m):
        zh = 2 * m + e
        flat = (2 * SEC, SEC)
        mid = dot3((lh[zh].reshape(flat), ll[zh].reshape(flat)), (wh[...], wl[...]), (1, 0))
        high, low = split(mid)
        parts = []
        for core in range(2):
            k = 2 * term_pair(zh, core) + core
            rows = slice(core * SEC, (core + 1) * SEC)
            parts.append((high[rows], low[rows], rh[s, k], rl[s, k]))
        (h0, l0, rh0, rl0), (h1, l1, rh1, rl1) = parts
        return dot3(
            (jnp.concatenate([h0, h1], 1), jnp.concatenate([l0, l1], 1)),
            (jnp.concatenate([rh0, rh1], 1), jnp.concatenate([rl0, rl1], 1)), (1, 1))

    for p in range(2):
        s = rem(p + xodd, 2)
        for e in (1 - odd, odd):
            inside = (row_at < ldims[x * Z + 2 * y + e]) & (col_at < rdims[(2 * c + s) * Z + z])
            for q in range(4):
                received(wbuf.at[e, s, pl.ds(q * PIECE, PIECE)], w_r.at[s, e, q])
            wh[...], wl[...] = split(jnp.where(inside, wbuf[e, s], 0.0))
            acc[s, e] = product(s, e, 0)
            for m in range(1, 4):
                acc[s, e] += product(s, e, m)
            acc[s, e] = jnp.where(inside, acc[s, e], 0.0)
            send(
                acc.at[s, e], out.at[2 * yodd + e], o_s.at[s, e], o_r.at[2 * yodd + e],
                device(2 * c + s, x, z, ypair), (x == y) & (c == ypair) & (xodd == s))
            if p == 0 and e is not odd:
                for n in (CHUNKS - 2, CHUNKS - 1):
                    arrive(n)
                lax.fori_loop(issued(CHUNKS - 1), 16, spread, 0)
                for n in (CHUNKS - 2, CHUNKS - 1):
                    prepare(n)

    for drain in drains:
        drain()
    for s in range(2):
        @pl.when(jnp.logical_not((x == y) & (c == ypair) & (xodd == s)))
        def _():
            for e in range(2):
                received(acc.at[s, e], o_s.at[s, e])

    def drain_wave(i, carry):
        part = wbuf.at[0, 0, pl.ds(0, PIECE)]
        pl.when(jnp.logical_not(w_self & (rem(i, 8) == 7)))(
            lambda: received(part, w_s.at[div(i, 8), rem(i, 8)]))
        return carry

    lax.fori_loop(0, 16, drain_wave, 0)

    def drain_ring(n, carry):
        part = lbuf.at[0, 0, pl.ds(0, HALF)]
        pl.when(n >= 2)(lambda: pltpu.make_async_copy(part, part, ring_s.at[n]).wait())
        pltpu.make_async_copy(part, part, sib_s.at[n]).wait()
        return carry

    lax.fori_loop(0, CHUNKS, drain_ring, 0)

    @pl.when(r_owner)
    def _():
        def drain_right(k, carry):
            for way in range(2):
                received(upper(0, 0), ra2_s.at[way, k])
            return carry
        lax.fori_loop(0, 8, drain_right, 0)

    for s in range(2):
        for d, first in ((1, 0), (3, 1)):
            @pl.when(distance(s) == d)
            def _():
                def drain_relay(i, carry):
                    received(upper(0, 0), ra3_s.at[s, 2 * i + first])
                    return carry
                lax.fori_loop(0, 4, drain_relay, 0)

    for j in range(4):
        received(out.at[j], o_r.at[j])


def shards(wave, left_env, right_env, left_dims, right_dims):
    dma = pltpu.SemaphoreType.DMA
    vmem, smem, hbm = pltpu.VMEM, pltpu.SMEM, pl.ANY
    return pl.pallas_call(
        kernel,
        out_shape=jax.ShapeDtypeStruct((4, SEC, SEC), F32),
        in_specs=[pl.BlockSpec(memory_space=smem)] * 2 + [pl.BlockSpec(memory_space=hbm)] * 3,
        out_specs=pl.BlockSpec(memory_space=hbm),
        scratch_shapes=[
            vmem((Z, 2, SEC, SEC), F32),
            vmem((2, 8, SEC, SEC), F32),
            vmem((2, 2, SEC, SEC), F32),
            vmem((Z, 2, SEC, SEC), BF16),
            vmem((Z, 2, SEC, SEC), BF16),
            vmem((SEC, SEC), BF16),
            vmem((SEC, SEC), BF16),
            vmem((2, 8, SEC, SEC), BF16),
            vmem((2, 8, SEC, SEC), BF16),
            vmem((2, 2, SEC, SEC), F32),
            dma((2,)), dma((CHUNKS,)), dma((CHUNKS,)), dma((CHUNKS,)), dma((CHUNKS,)),
            dma((4,)), dma((2, 8)), dma((2, 8)), dma((2, 8)), dma((4,)), dma((2, 2)), dma((3, 2)), dma((3, 2)),
            dma((2, 8)), dma((2, 2, 4)), dma((2, 2)), dma((4,)),
        ],
        compiler_params=pltpu.CompilerParams(
            collective_id=0, has_side_effects=True, vmem_limit_bytes=60 * 2 ** 20),
        cost_estimate=pl.CostEstimate(
            flops=6 * 64 * SEC ** 3, bytes_accessed=4 * 2 ** 20, transcendentals=0),
        name="two_site",
    )(left_dims, right_dims, wave, left_env, right_env).reshape(4 * SEC, SEC)


def solution(mesh):
    placed = (P("blk", None), P("term", "blk", None, None), P("term", "blk", None, None), P(), P())
    return jax.shard_map(
        shards, mesh=mesh, in_specs=placed, out_specs=P("term", "blk"), check_vma=False
    )
```
